32 devices in a mesh: seq: 16 (over z, x, core), chan: 2 (over y).
Axes of the slice: x: 2, y: 2, z: 4, core: 2. Of those that a mesh axis runs over, the one named last changes fastest.
Arguments:
- inputs: bfloat16 [131072, 2048], P('seq', 'chan'), may hold values from -6 to 6
- twiddle: float32 [256, 512], P('seq'), may hold values from -4 to 4
- right_factor: bfloat16 [512, 512], replicated, may hold values from -0.25 to 0.25
- left_factor: bfloat16 [256, 256], replicated, may hold values from -0.375 to 0.375
- blocks: bfloat16 [2048, 512], P('chan'), may hold values from -0.25 to 0.25
- block_mixer: float32 [512, 4, 4], replicated, may hold values from -3 to 3
- out_grad: bfloat16 [131072, 2048], P('seq', 'chan'), may hold values from -6 to 6
Outputs:
- output: bfloat16 [131072, 2048], P('seq', 'chan')
- input_grad: bfloat16 [131072, 2048], P('seq', 'chan')
The draws below stay inside these ranges and needn't reach their ends.
All inputs are finite; a program needn't handle non-finite values.
Results may differ from the reference program's by a relative error of at most 0.0076.
Values may be sent and summed in bfloat16 or wider, within the bound.
A program may use at most 256 MiB of HBM per device.

```python
import jax
import jax.numpy as jnp
from jax import lax

SA = 256
SB = 512
D = 2048
BW = 512
NBLK = 4
SEQ_LEN = 131072


def block_levels(own_key, dims, cuts, low, high):
    level, own = 1.0, jax.random.fold_in(own_key, 6)
    for axis_at, shards_of in cuts:
        steps = jnp.exp(jax.random.uniform(jax.random.fold_in(own, axis_at), (shards_of,), jnp.float32, low / len(cuts), high / len(cuts)))
        level = level * jnp.repeat(steps, dims[axis_at] // shards_of).reshape([-1 if axis == axis_at else 1 for axis in range(len(dims))])
    return level


def scatter_about(rng, shape, scale, most, shards=(), held_as=jnp.bfloat16):
    result = jax.random.normal(rng, shape, jnp.float32) * scale
    if len(shards) > 0:
        result = block_levels(rng, shape, shards, -0.22, 0.18) * result
    return jnp.clip(result, min=-most, max=most).astype(held_as)


def setup_inputs(seed: int = 0) -> dict:
    splits = jax.random.split(jax.random.key(seed), 8)
    inputs = scatter_about(splits[0], (SEQ_LEN, D), 1.0, 6.0, ((0, 16), (1, 2)))
    twiddle = scatter_about(splits[1], (SA, SB), 1.0, 4.0, ((0, 16),), jnp.float32)
    right_factor = scatter_about(splits[2], (SB, SB), SB ** -0.5, 0.25)
    left_factor = scatter_about(splits[3], (SA, SA), SA ** -0.5, 0.375)
    blocks = scatter_about(splits[4], (D, BW), BW ** -0.5, 0.25, ((0, 2),))
    block_mixer = scatter_about(splits[5], (BW, NBLK, NBLK), NBLK ** -0.5, 3.0, (), jnp.float32)
    out_grad = scatter_about(splits[6], (SEQ_LEN, D), 1.0, 6.0, ((0, 16), (1, 2)))
    return dict(inputs=inputs, twiddle=twiddle, right_factor=right_factor, left_factor=left_factor, blocks=blocks, block_mixer=block_mixer, out_grad=out_grad)


def reference(inputs, twiddle, right_factor, left_factor, blocks, block_mixer, out_grad):
    group_size = min(D, 256)
    group_count = D // group_size
    right_wide = right_factor.astype(jnp.float32)
    left_wide = left_factor.astype(jnp.float32)

    def to_groups(array):
        return array.reshape(SA, SB, group_count, group_size).transpose(2, 0, 1, 3)

    def from_groups(array):
        return array.transpose(1, 2, 0, 3).reshape(SA * SB, D)

    def forward_seq(values):
        first_section = jnp.einsum('jb,abc->ajc', right_wide, values.astype(jnp.float32))
        twisted = (first_section * twiddle[:, :, None]).astype(jnp.bfloat16)
        return jnp.einsum('ia,ajc->ijc', left_wide, twisted.astype(jnp.float32)).astype(jnp.bfloat16)

    mixed = from_groups(lax.map(forward_seq, to_groups(inputs)))
    block_table = blocks.reshape(NBLK, BW, BW).astype(jnp.float32)

    def channel_row(pieces):
        x_row, mixed_row, grad_row = pieces
        split = x_row.reshape(SB, NBLK, BW).astype(jnp.float32)
        middle = jnp.einsum('bpq,pkq->bpk', split, block_table).astype(jnp.bfloat16)
        gate = jnp.einsum('bpk,kop->bok', middle.astype(jnp.float32), block_mixer,
                          precision=lax.Precision.HIGHEST).reshape(SB, D).astype(jnp.bfloat16)
        output_row = (gate.astype(jnp.float32) * mixed_row.astype(jnp.float32)).astype(jnp.bfloat16)
        grad_gate = (grad_row.astype(jnp.float32) * mixed_row.astype(jnp.float32)).astype(jnp.bfloat16)
        grad_mixed = (grad_row.astype(jnp.float32) * gate.astype(jnp.float32)).astype(jnp.bfloat16)
        grad_middle = jnp.einsum('bok,kop->bpk', grad_gate.reshape(SB, NBLK, BW).astype(jnp.float32),
                                 block_mixer, precision=lax.Precision.HIGHEST).astype(jnp.bfloat16)
        chan_grad = jnp.einsum('bpk,pkq->bpq', grad_middle.astype(jnp.float32),
                               block_table).reshape(SB, D).astype(jnp.bfloat16)
        return output_row, chan_grad, grad_mixed

    output, chan_grad, grad_mixed = lax.map(
        channel_row, (inputs.reshape(SA, SB, D), mixed.reshape(SA, SB, D), out_grad.reshape(SA, SB, D)))

    def backward_seq(values):
        grad_twisted = jnp.einsum('ia,ijc->ajc', left_wide, values.astype(jnp.float32)).astype(jnp.bfloat16)
        grad_first = (grad_twisted.astype(jnp.float32) * twiddle[:, :, None]).astype(jnp.bfloat16)
        return jnp.einsum('jb,ajc->abc', right_wide, grad_first.astype(jnp.float32))

    seq_grad = from_groups(lax.map(backward_seq, to_groups(grad_mixed.reshape(SA * SB, D))))
    input_grad = (seq_grad + chan_grad.reshape(SA * SB, D).astype(jnp.float32)).astype(jnp.bfloat16)
    return output.reshape(SA * SB, D), input_grad
```

```python
import jax
import jax.numpy as jnp
from jax import lax
from jax.sharding import PartitionSpec as P

F32, BF16 = jnp.float32, jnp.bfloat16


def seq_pass(values, left_matrix, after=None):
    mixed_cols = jnp.einsum(
        "ia,ajc->ijc",
        left_matrix,
        lax.all_to_all(values, "seq", split_axis=1, concat_axis=0, tiled=True),
        preferred_element_type=F32,
    ).astype(BF16)
    if after is not None:
        mixed_cols, _ = lax.optimization_barrier((mixed_cols, after))
    return lax.all_to_all(mixed_cols, "seq", split_axis=0, concat_axis=1, tiled=True)


def send_back(values):
    return (
        lax.all_to_all(values[0], "chan", split_axis=2, concat_axis=1, tiled=True),
        lax.all_to_all(values[1], "chan", split_axis=2, concat_axis=1, tiled=True),
    )


def gate_of(values, rows_all, block_mixer):
    row_count, length, full_width = values.shape
    block_width = rows_all.shape[1]
    block_count = full_width // block_width
    block_table = rows_all.reshape(block_count, block_width, block_width)
    split = values.reshape(row_count, length, block_count, block_width)
    middle = jnp.einsum(
        "nbpq,pkq->nbpk", split, block_table, preferred_element_type=jnp.float32
    ).astype(jnp.bfloat16)
    gate = jnp.einsum(
        "nbpk,kop->nbok", middle.astype(jnp.float32), block_mixer, precision=lax.Precision.HIGHEST
    )
    return gate.reshape(row_count, length, full_width).astype(jnp.bfloat16)


def grad_of(values, rows_all, block_mixer):
    row_count, length, full_width = values.shape
    block_width = rows_all.shape[1]
    block_count = full_width // block_width
    block_table = rows_all.reshape(block_count, block_width, block_width)
    split = values.reshape(row_count, length, block_count, block_width).astype(jnp.float32)
    grad_middle = jnp.einsum(
        "nbok,kop->nbpk", split, block_mixer, precision=lax.Precision.HIGHEST
    ).astype(jnp.bfloat16)
    chan_grad = jnp.einsum(
        "nbpk,pkq->nbpq", grad_middle, block_table, preferred_element_type=jnp.float32
    )
    return chan_grad.reshape(row_count, length, full_width).astype(jnp.bfloat16)


def split_blocks(inputs, twiddle, right_factor, left_factor, blocks, block_mixer, out_grad):
    outer_rows, inner_len = twiddle.shape
    local_chan = inputs.shape[1]
    values = inputs.reshape(outer_rows, inner_len, local_chan)
    grad_values = out_grad.reshape(outer_rows, inner_len, local_chan)
    rows_all = lax.all_gather(blocks, "chan", axis=0, tiled=True)
    first_section = jnp.einsum(
        "jb,abc->ajc", right_factor, values, preferred_element_type=jnp.float32
    )
    twisted = (first_section * twiddle[:, :, None]).astype(jnp.bfloat16)
    mixed = seq_pass(twisted, left_factor)
    mixed_wide = mixed.astype(jnp.float32)
    grad_wide = grad_values.astype(jnp.float32)
    grad_gate = (grad_wide * mixed_wide).astype(jnp.bfloat16)
    gate, chan_grad = send_back(
        (
            gate_of(
                lax.all_to_all(values, "chan", split_axis=1, concat_axis=2, tiled=True),
                rows_all,
                block_mixer,
            ),
            grad_of(
                lax.all_to_all(grad_gate, "chan", split_axis=1, concat_axis=2, tiled=True),
                rows_all,
                block_mixer,
            ),
        )
    )
    gate_wide = gate.astype(jnp.float32)
    output = (gate_wide * mixed_wide).astype(jnp.bfloat16)
    grad_mixed = (grad_wide * gate_wide).astype(jnp.bfloat16)
    grad_twisted = seq_pass(grad_mixed, left_factor.T)
    grad_first = (grad_twisted.astype(jnp.float32) * twiddle[:, :, None]).astype(jnp.bfloat16)
    seq_grad = jnp.einsum(
        "jb,ajc->abc", right_factor, grad_first, preferred_element_type=jnp.float32
    )
    input_grad = (seq_grad + chan_grad.astype(jnp.float32)).astype(jnp.bfloat16)
    total_rows = outer_rows * inner_len
    return (output.reshape(total_rows, local_chan), input_grad.reshape(total_rows, local_chan))


def local(inputs, twiddle, right_factor, left_factor, blocks, block_mixer, out_grad):
    outer_rows, inner_len = twiddle.shape
    local_chan = inputs.shape[1]
    width = blocks.shape[1]
    if local_chan % width:
        return split_blocks(
            inputs, twiddle, right_factor, left_factor, blocks, block_mixer, out_grad
        )
    parts = local_chan // width
    chan_size = lax.axis_size("chan")
    me = lax.axis_index("chan")
    values = inputs.reshape(outer_rows, inner_len, local_chan)
    grad_values = out_grad.reshape(outer_rows, inner_len, local_chan)
    x = [values[:, :, i * width:(i + 1) * width] for i in range(parts)]
    grad = [grad_values[:, :, i * width:(i + 1) * width] for i in range(parts)]
    table = [blocks[i * width:(i + 1) * width] for i in range(parts)]
    number = [[(me + chan_size - r) % chan_size * parts + i for i in range(parts)] for r in range(chan_size)]

    def from_all(arrays):
        held = [arrays]
        for r in range(1, chan_size):
            perm = [(d, (d + r) % chan_size) for d in range(chan_size)]
            held.append([lax.ppermute(a, "chan", perm) for a in arrays])
        return held

    def mix(held, coefs):
        total = 0.0
        for r in range(chan_size):
            for i in range(parts):
                row = lax.dynamic_index_in_dim(coefs, number[r][i], axis=0, keepdims=False)
                total = total + held[r][i].astype(F32) * row[None, None, :]
        return total.astype(BF16)

    def mixer_row(axis, index):
        return lax.dynamic_index_in_dim(jnp.transpose(block_mixer, (1, 2, 0)), index, axis=axis, keepdims=False)

    middle = [
        jnp.einsum("nbq,kq->nbk", x[i], table[i], preferred_element_type=F32).astype(BF16)
        for i in range(parts)
    ]
    middle_all = from_all(middle)
    mixed = []
    for i in range(parts):
        first_section = jnp.einsum("jb,abc->ajc", right_factor, x[i], preferred_element_type=F32)
        twisted = (first_section * twiddle[:, :, None]).astype(BF16)
        mixed.append(seq_pass(twisted, left_factor))
    gate = [mix(middle_all, mixer_row(0, number[0][i])) for i in range(parts)]

    grad_gate = [(grad[i].astype(F32) * mixed[i].astype(F32)).astype(BF16) for i in range(parts)]
    grad_gate_all = from_all(grad_gate)
    output, input_grad = [], []
    seq_grad = []
    for i in range(parts):
        gate_wide = gate[i].astype(F32)
        output.append((gate_wide * mixed[i].astype(F32)).astype(BF16))
        grad_mixed = (grad[i].astype(F32) * gate_wide).astype(BF16)
        grad_twisted = seq_pass(grad_mixed, left_factor.T, grad_gate[i])
        grad_first = (grad_twisted.astype(F32) * twiddle[:, :, None]).astype(BF16)
        seq_grad.append(jnp.einsum("jb,ajc->abc", right_factor, grad_first, preferred_element_type=F32))
    for i in range(parts):
        grad_middle = mix(grad_gate_all, mixer_row(1, number[0][i]))
        chan_grad = jnp.einsum("nbk,kq->nbq", grad_middle, table[i], preferred_element_type=F32).astype(BF16)
        input_grad.append((seq_grad[i] + chan_grad.astype(F32)).astype(BF16))
    total_rows = outer_rows * inner_len
    return (
        jnp.concatenate(output, axis=2).reshape(total_rows, local_chan),
        jnp.concatenate(input_grad, axis=2).reshape(total_rows, local_chan),
    )


def solution(mesh):
    return jax.shard_map(
        local,
        mesh=mesh,
        in_specs=(
            P("seq", "chan"),
            P("seq", None),
            P(),
            P(),
            P("chan", None),
            P(),
            P("seq", "chan"),
        ),
        out_specs=(P("seq", "chan"), P("seq", "chan")),
        check_vma=False,
    )
```
